512 devices in a mesh: dp: 4 (over z_lo), expert: 128 (over y, x, z_hi, core).
Axes of the slice: x: 4, y: 4, z: 16 (z_hi: 4, z_lo: 4; z = z_hi * 4 + z_lo), core: 2. Of those that a mesh axis runs over, the one named last changes fastest.
Arguments:
- hidden_in: bfloat16 [2, 8192, 2048], P(None, ('dp', 'expert')), may hold values from -6 to 6
- cotangent: bfloat16 [2, 8192, 2048], P(None, ('dp', 'expert')), may hold values from -6 to 6
- expert_ids: int32 [2, 8192, 8], P(None, ('dp', 'expert')), may hold values from 0 to 127, all different within a row; in each aligned block of 16 rows (0 to 15, 16 to 31, ..., all dimensions but the last counted through in order) at most 2 rows name the same one
- route_prob: float32 [2, 8192, 8], P(None, ('dp', 'expert')), may hold values from 0.05 to 1
- swap_flags: int32 [64], replicated, may hold values 0 or 1
- gate_up: bfloat16 [128, 2048, 2, 384], P('expert', 'dp'), may hold values from -0.125 to 0.125
- down_t: bfloat16 [128, 2048, 384], P('expert', 'dp'), may hold values from -0.3125 to 0.3125
Outputs:
- hidden_out: bfloat16 [2, 8192, 2048], P(None, ('dp', 'expert'))
- input_grad: bfloat16 [2, 8192, 2048], P(None, ('dp', 'expert'))
- resident_gate_up: bfloat16 [128, 2048, 2, 384], P('expert', 'dp')
- resident_down: bfloat16 [128, 2048, 384], P('expert', 'dp')
The draws below stay inside these ranges and needn't reach their ends.
Inputs may be any that keep to these rules, and one draw needn't show every extreme that they name: `expert_ids`: within one microbatch the 16 tokens of one device name any one expert at most 2 times, a bound that some block reaches.
All inputs are finite; a program needn't handle non-finite values.
Results may differ from the reference program's by a relative error of at most 0.0064.
Values may be sent and summed in bfloat16 or wider, within the bound.
No kernel may reach another device: no remote copies, remote signals or barrier semaphores. Data moves between devices by JAX's collectives and lax.ppermute only.
A program may use at most 64 MiB of HBM per device.

```python
import math
import jax
import jax.numpy as jnp
import numpy as np
from jax import lax

D = 2048
HID = 384
TOP = 8
MICRO = 2
TOK = 16
EXPERTS = 128
SRC_CAP = 2
TOKENS = 8192
N_DP = 4
N_EXPERT = 128


def set_ends(entries, rng, low, high):
    place = [jax.random.randint(jax.random.fold_in(rng, axis), (), 0, length) for axis, length in enumerate(entries.shape)]
    longest = entries.shape.index(max(entries.shape))
    next_to = place[:longest] + [(place[longest] + 1) % entries.shape[longest]] + place[longest + 1:]
    return entries.at[tuple(place)].set(low).at[tuple(next_to)].set(high)


def steps_of(own_key, extent, split, low, top_value):
    gain = 1.0
    for dim, parts in split:
        heights = jax.random.uniform(jax.random.fold_in(jax.random.fold_in(own_key, 6), dim), (parts,), jnp.float32, low / len(split), top_value / len(split))
        gain = gain * jnp.repeat(jnp.exp(heights), extent[dim] // parts).reshape((-1,) + (1,) * (len(extent) - 1 - dim))
    return gain


def deal_out(key, own, number, rows, amount, top, reach, slope):
    sequence = jax.random.permutation(key, amount)
    packed, common = shares(amount, rows * top, reach, slope, True), shares(amount, rows * top, reach, slope, False)
    places = jnp.arange(amount)

    def named(tallies, rotation):
        used = int((tallies > 0).sum())
        fixed = max(1, used // 4)
        moved = fixed + (places - fixed + rotation * (used - fixed)) % max(1, amount - fixed)
        return jnp.zeros((amount,), jnp.int32).at[sequence[jnp.where(places < fixed, places, moved)]].set(jnp.asarray(tallies, jnp.int32))

    tallies = jnp.where(number % 4 == 0, named(packed, number // 4), named(common, number - number // 4 - 1))
    mixed = jax.random.permutation(jax.random.fold_in(own, 3), amount)
    source_of, sink = mixed[0:amount // 2 * 2:2], mixed[1:amount // 2 * 2:2]
    slack = jnp.minimum(tallies[source_of] - 1, reach - tallies[sink]) // 2
    slack = jnp.where((source_of == sequence[0]) | (sink == sequence[0]) | (tallies[sink] == 0), 0, jnp.maximum(slack, 0))
    moved = jax.random.randint(jax.random.fold_in(own, 4), (amount // 2,), 0, 1 << 20) % (slack + 1)
    tallies = tallies.at[source_of].add(-moved).at[sink].add(moved)
    labels = jnp.searchsorted(jnp.cumsum(tallies), jnp.arange(rows * top), side="right").astype(jnp.int32)
    listing = labels.reshape(top, rows).T
    listing = listing[jax.random.permutation(jax.random.fold_in(own, 1), rows)]
    rotation = jax.random.randint(jax.random.fold_in(own, 2), (rows, 1), 0, top)
    return jnp.take_along_axis(listing, (jnp.arange(top)[None, :] + rotation) % top, axis=1)


def shares(amount, total, most, lean, full):
    weights = [(1 << 20) // math.isqrt(rank ** lean) + 1 for rank in range(1, amount + 1)]
    largest = most if full else min(most, max(-(-total // amount), total * weights[0] // sum(weights)))
    least = 1 if total - largest >= amount - 1 else 0
    given, rest = [largest] + [least] * (amount - 1), total - largest - least * (amount - 1)
    while rest > 0:
        movable = [i for i in range(1, amount) if given[i] < largest] or [i for i in range(1, amount) if given[i] < most]
        mass, remaining = sum([weights[i] for i in movable]), rest
        for i in movable:
            addition = min(most - given[i], max(1, remaining * weights[i] // mass), rest)
            given[i] = given[i] + addition
            rest = rest - addition
    return np.array(given)


def bell_draw(own_key, shape, deviation, reach, cuts=(), held_as=jnp.bfloat16):
    factor_of = steps_of(own_key, shape, cuts, -0.22, 0.18) if cuts else 1.0
    array = jax.random.normal(own_key, shape, jnp.float32) * deviation * factor_of
    return jnp.minimum(jnp.maximum(array, -reach), reach).astype(held_as)


def setup_inputs(seed: int = 0) -> dict:
    arg_keys = jax.random.split(jax.random.key(seed), 8)
    hidden_in = bell_draw(arg_keys[0], (MICRO, TOKENS, D), 1.0, 6.0, ((1, 512),))
    cotangent = bell_draw(arg_keys[1], (MICRO, TOKENS, D), 1.0, 6.0, ((1, 512),))
    expert_ids_keys = jax.random.split(jax.random.fold_in(arg_keys[2], 1), MICRO * TOKENS // TOK)
    expert_ids_turns = jax.random.permutation(jax.random.fold_in(arg_keys[2], 3), MICRO * TOKENS // TOK)
    expert_ids = jax.vmap(lambda own, number: deal_out(jax.random.fold_in(arg_keys[2], 2), own, number, TOK, EXPERTS, TOP, SRC_CAP, 2))(expert_ids_keys, expert_ids_turns).reshape((MICRO, TOKENS, TOP))
    route_prob = jnp.clip(jnp.exp(math.log(1.0) - 2.9957323 * jax.random.uniform(arg_keys[3], (MICRO, TOKENS, TOP), jnp.float32) ** steps_of(arg_keys[3], (MICRO, TOKENS, TOP), ((1, 512),), -0.2, 0.2)), 0.05, 1.0)
    swap_flags = set_ends((jax.random.randint(arg_keys[4], (EXPERTS // 2,), 0, 2) < 1).astype(jnp.int32), jax.random.fold_in(arg_keys[4], 1), 0, 1)
    gate_up = bell_draw(arg_keys[5], (EXPERTS, D, 2, HID), D ** -0.5, 0.125, ((0, 128), (1, 4)))
    down_t = bell_draw(arg_keys[6], (EXPERTS, D, HID), HID ** -0.5, 0.3125, ((0, 128), (1, 4)))
    return {"hidden_in": hidden_in, "cotangent": cotangent, "expert_ids": expert_ids, "route_prob": route_prob, "swap_flags": swap_flags, "gate_up": gate_up, "down_t": down_t}


def expert_forward(row_block, gate_matrix, down_matrix):
    hidden_width = down_matrix.shape[1]
    projected = jnp.dot(row_block, gate_matrix, preferred_element_type=jnp.float32)
    gate_part = projected[:, :hidden_width]
    upper_part = projected[:, hidden_width:]
    hidden = (jax.nn.silu(gate_part) * upper_part).astype(jnp.bfloat16)
    output = lax.dot_general(hidden, down_matrix, (((1,), (1,)), ((), ())), preferred_element_type=jnp.float32)
    return output.astype(jnp.bfloat16), projected


def expert_backward(grad_block, projected, gate_matrix, down_matrix):
    hidden_width = down_matrix.shape[1]
    gate_part = projected[:, :hidden_width]
    upper_part = projected[:, hidden_width:]
    d_hidden = jnp.dot(grad_block, down_matrix, preferred_element_type=jnp.float32)
    sigmoid_gate = jax.nn.sigmoid(gate_part)
    d_gate = (d_hidden * upper_part * sigmoid_gate * (1.0 + gate_part * (1.0 - sigmoid_gate))).astype(jnp.bfloat16)
    d_upper = (d_hidden * gate_part * sigmoid_gate).astype(jnp.bfloat16)
    d_joined = jnp.concatenate([d_gate, d_upper], axis=1)
    d_rows = lax.dot_general(d_joined, gate_matrix, (((1,), (1,)), ((), ())), preferred_element_type=jnp.float32)
    return d_rows.astype(jnp.bfloat16)


def reference(hidden_in, cotangent, expert_ids, route_prob, swap_flags, gate_up, down_t):
    capacity = N_DP * N_EXPERT * SRC_CAP
    expert_range = jnp.arange(EXPERTS, dtype=jnp.int32)
    outputs = []
    gradients = []
    for microbatch in range(hidden_in.shape[0]):
        tokens_now = hidden_in[microbatch]
        grads_now = cotangent[microbatch]
        weights_now = route_prob[microbatch]
        flat_ids = expert_ids[microbatch].reshape(-1).astype(jnp.int32)
        sorted_rows = jnp.argsort(flat_ids, stable=True).astype(jnp.int32)
        sorted_rows = jnp.concatenate([sorted_rows, jnp.zeros((capacity,), jnp.int32)])
        counts = jnp.sum((flat_ids[None, :] == expert_range[:, None]).astype(jnp.int32), axis=1).astype(jnp.int32)
        starts = (jnp.cumsum(counts) - counts).astype(jnp.int32)
        zero_field = jnp.zeros(tokens_now.shape, jnp.float32)

        def one_expert(expert_id, carried):
            out_total, grad_total = carried
            row_index = lax.dynamic_slice(sorted_rows, (starts[expert_id].astype(jnp.int32),), (capacity,))
            valid_rows = jnp.arange(capacity, dtype=jnp.int32) < counts[expert_id]
            token_index = row_index // TOP
            top_index = row_index % TOP
            row_weight = weights_now[token_index, top_index]
            row_grads = (row_weight[:, None] * grads_now[token_index].astype(jnp.float32)).astype(jnp.bfloat16)
            gate_matrix = lax.dynamic_index_in_dim(gate_up, expert_id, 0, keepdims=False).reshape(D, 2 * HID)
            down_matrix = lax.dynamic_index_in_dim(down_t, expert_id, 0, keepdims=False)
            expert_out, projected = expert_forward(tokens_now[token_index], gate_matrix, down_matrix)
            row_input = expert_backward(row_grads, projected, gate_matrix, down_matrix)
            kept_weight = jnp.where(valid_rows, row_weight, 0.0)
            out_total = out_total.at[token_index].add(kept_weight[:, None] * expert_out.astype(jnp.float32))
            grad_total = grad_total.at[token_index].add(jnp.where(valid_rows[:, None], row_input.astype(jnp.float32), 0.0))
            return out_total, grad_total

        out_total, grad_total = lax.fori_loop(jnp.int32(0), jnp.int32(EXPERTS), one_expert, (zero_field, zero_field))
        outputs.append(out_total.astype(jnp.bfloat16))
        gradients.append(grad_total.astype(jnp.bfloat16))
    half_axis = EXPERTS // 2
    device_range = jnp.arange(EXPERTS, dtype=jnp.int32)
    flag_of = swap_flags[device_range % half_axis]
    holder = jnp.where(flag_of == 1, device_range ^ half_axis, device_range).astype(jnp.int32)
    return (jnp.stack(outputs), jnp.stack(gradients), gate_up[holder], down_t[holder])
```

```python
import jax
import jax.numpy as jnp
from jax import lax
from jax.sharding import Mesh, PartitionSpec as P

EXPERT = ("y", "x", "z", "c")
PLANE = ("y", "x", "c")
BF = jnp.bfloat16
F32 = jnp.float32


def along_z(value, shift):
    count = lax.axis_size("z")
    return lax.ppermute(value, "z", [(i, (i + shift) % count) for i in range(count)])


def local(hidden_in, cotangent, expert_ids, route_prob, swap_flags, gate_up, down_t):
    micro, tok, width = hidden_in.shape
    top = expert_ids.shape[2]
    hid = down_t.shape[2]
    nz = lax.axis_size("z")
    ny = lax.axis_size("y")
    plane = ny * lax.axis_size("x") * 2
    my_z = lax.axis_index("z")
    my_y = lax.axis_index("y")
    half = ny * lax.axis_size("x") * nz
    my_index = lax.axis_index(EXPERT)

    flag = jnp.sum(jnp.where(jnp.arange(half, dtype=jnp.int32) == my_index % half, swap_flags, 0))
    pairs = [(i, i ^ (ny // 2)) for i in range(ny)]
    other_gate = lax.ppermute(gate_up, "y", pairs)
    other_down = lax.ppermute(down_t, "y", pairs)
    resident_gate = jnp.where(flag == 1, other_gate, gate_up)
    resident_down = jnp.where(flag == 1, other_down, down_t)

    mine = jnp.stack([hidden_in, cotangent])
    facts = jnp.concatenate([expert_ids.astype(F32), route_prob], axis=2)
    facts = jnp.stack([facts] + [along_z(facts, s) for s in range(1, nz)])
    column = jnp.stack([mine] + [along_z(mine, s) for s in range(1, nz)])

    weights = jnp.concatenate([gate_up.reshape(-1, 2 * hid), down_t.reshape(-1, hid)], axis=1)
    weights = lax.all_gather(weights, "dp", axis=0, tiled=True)
    gate_matrix = weights[:, : 2 * hid]
    down_matrix = weights[:, 2 * hid :]

    ids = facts[..., :top].astype(jnp.int32)
    prob = facts[..., top:]
    core = ids % 2
    place = (ids // (2 * nz)) * 2 + core
    place = jnp.where((ids // 2) % nz == my_z, place, -1)
    hit = place[..., None] == jnp.arange(plane, dtype=jnp.int32)
    member = jnp.any(hit, axis=3)
    weight = jnp.sum(jnp.where(hit, prob[..., None], 0.0), axis=3)
    below = jnp.tril(jnp.ones((tok, tok), F32), -1)
    earlier = jnp.einsum("ut,smtd->smud", below, member.astype(F32))
    rank = jnp.arange(2, dtype=jnp.int32).astype(F32)
    pick = member[..., None] & (earlier[..., None] == rank)
    pick = pick.astype(F32)
    slot_weight = jnp.einsum("smtdr,smtd->dmsr", pick, weight)

    pick_b = pick.astype(BF)
    rows_x = jnp.einsum("smtdr,smtw->dmsrw", pick_b, column[:, 0], preferred_element_type=F32).astype(BF)
    rows_g = jnp.einsum("smtdr,smtw->dmsrw", pick_b, column[:, 1], preferred_element_type=F32)
    rows_g = (rows_g * slot_weight[..., None]).astype(BF)
    count = micro * nz * 2
    rows = jnp.concatenate(
        [rows_x.reshape(plane, count, width), rows_g.reshape(plane, count, width)], axis=1
    )
    rows = lax.all_to_all(rows, PLANE, 0, 0, tiled=True)
    tokens_now = rows[:, :count].reshape(plane * count, width)
    grads_now = rows[:, count:].reshape(plane * count, width)

    projected = jnp.dot(tokens_now, gate_matrix, preferred_element_type=F32)
    gate_part = projected[:, :hid]
    upper_part = projected[:, hid:]
    sig = jax.nn.sigmoid(gate_part)
    hidden = (gate_part * sig * upper_part).astype(BF)
    last = (((1,), (1,)), ((), ()))
    expert_out = lax.dot_general(hidden, down_matrix, last, preferred_element_type=F32).astype(BF)
    d_hidden = jnp.dot(grads_now, down_matrix, preferred_element_type=F32)
    d_gate = (d_hidden * upper_part * sig * (1.0 + gate_part * (1.0 - sig))).astype(BF)
    d_upper = (d_hidden * gate_part * sig).astype(BF)
    d_joined = jnp.concatenate([d_gate, d_upper], axis=1)
    row_input = lax.dot_general(d_joined, gate_matrix, last, preferred_element_type=F32).astype(BF)

    back = jnp.concatenate(
        [expert_out.reshape(plane, count, width), row_input.reshape(plane, count, width)], axis=1
    )
    back = lax.all_to_all(back, PLANE, 0, 0, tiled=True)
    back_out = back[:, :count].reshape(plane, micro, nz, 2, width)
    back_grad = back[:, count:].reshape(plane, micro, nz, 2, width)

    scaled = pick * weight[..., None]
    scaled_high = scaled.astype(BF)
    scaled_low = (scaled - scaled_high.astype(F32)).astype(BF)
    form = "smtdr,dmsrw->smtw"
    part_out = jnp.einsum(form, scaled_high, back_out, preferred_element_type=F32) + jnp.einsum(
        form, scaled_low, back_out, preferred_element_type=F32
    )
    part_grad = jnp.einsum(form, pick_b, back_grad, preferred_element_type=F32)
    part = jnp.stack([part_out, part_grad], axis=1)
    total = part[0]
    for s in range(1, nz):
        total = total + along_z(part[s].astype(BF), -s).astype(F32)
    total = total.astype(BF)
    return (total[0], total[1], resident_gate, resident_down)


def solution(mesh):
    devices = mesh.devices.reshape(4, 4, 4, 4, 2)
    fine = Mesh(devices, ("dp", "y", "x", "z", "c"))
    tokens = P(None, ("dp",) + EXPERT, None)
    placed = (
        tokens,
        tokens,
        tokens,
        tokens,
        P(),
        P(EXPERT, "dp", None, None),
        P(EXPERT, "dp", None),
    )
    return jax.shard_map(
        local,
        mesh=fine,
        in_specs=placed,
        out_specs=(tokens, tokens, P(EXPERT, "dp", None, None), P(EXPERT, "dp", None)),
        check_vma=False,
    )
```

```python
import functools

import jax
import jax.numpy as jnp
from jax import lax
from jax.experimental import pallas as pl
from jax.experimental.pallas import tpu as pltpu
from jax.sharding import Mesh, PartitionSpec as P

EXPERT = ("y", "x", "z", "c")
PLANE = ("y", "x", "c")
BF = jnp.bfloat16
F32 = jnp.float32
STEP = 512
MORE = 128
ROWS = 256
GRANT = 60 << 20
LAST = (((1,), (1,)), ((), ()))


def along_z(value, shift):
    count = lax.axis_size("z")
    return lax.ppermute(value, "z", [(i, (i + shift) % count) for i in range(count)])


def cost(flops, size):
    return pl.CostEstimate(flops=flops, bytes_accessed=size, transcendentals=0)


def select_body(place_ref, f0, f1, f2, f3, a0, a1, x2, g2, a3, rows_ref, back_ref, high_ref, low_ref, pick_ref, scale_ref):
    n, slots = back_ref.shape
    half = n // 4

    @pl.when(pl.program_id(0) == 0)
    def _():
        facts = jnp.concatenate([f[...] for f in (f0, f1, f2, f3)], axis=0).astype(F32)
        ids = facts[:, 0:8].astype(jnp.int32)
        prob = facts[:, 8:16] + facts[:, 16:24] + facts[:, 24:32]
        place = jnp.where(((ids >> 1) & 3) == place_ref[0], ((ids >> 3) << 1) + (ids & 1), -1)
        col = lax.broadcasted_iota(jnp.int32, (n, slots), 1)
        row = lax.broadcasted_iota(jnp.int32, (n, slots), 0)
        dest = col >> 4
        hit = jnp.zeros((n, slots), jnp.bool_)
        weight = jnp.zeros((n, slots), F32)
        for k in range(8):
            same = place[:, k : k + 1] == dest
            hit = hit | same
            weight = jnp.where(same, prob[:, k : k + 1], weight)
        r2 = lax.broadcasted_iota(jnp.int32, (n, n), 0)
        c2 = lax.broadcasted_iota(jnp.int32, (n, n), 1)
        below = ((c2 < r2) & ((c2 >> 4) == (r2 >> 4))).astype(F32).astype(BF)
        earlier = jnp.dot(below, hit.astype(F32).astype(BF), preferred_element_type=F32)
        block = ((row >> 5) == ((col >> 1) & 3)) & (((row >> 4) & 1) == ((col >> 3) & 1))
        pick = hit & block & (earlier == (col & 1).astype(F32))
        pick_f = pick.astype(F32)
        scaled = jnp.where(pick, weight, 0.0)
        back_ref[...] = pick_f.astype(BF)
        high = scaled.astype(BF)
        high_ref[...] = high
        low_ref[...] = (scaled - high.astype(F32)).astype(BF)
        pick_ref[...] = jnp.transpose(pick_f).astype(BF)
        scale_ref[...] = jnp.sum(jnp.transpose(scaled), axis=1, keepdims=True)

    pick = pick_ref[...]
    shape = (rows_ref.shape[0], rows_ref.shape[2], rows_ref.shape[3])
    tokens = jnp.concatenate([a0[:half], a1[:half], x2[...], a3[:half]], axis=0)
    rows = jnp.dot(pick, tokens, preferred_element_type=F32)
    rows_ref[:, 0] = rows.astype(BF).reshape(shape)
    tokens = jnp.concatenate([a0[half:], a1[half:], g2[...], a3[half:]], axis=0)
    rows = jnp.dot(pick, tokens, preferred_element_type=F32)
    rows_ref[:, 1] = (rows * scale_ref[...]).astype(BF).reshape(shape)


def select(place, mine, up, far, down, plane, count):
    both = mine.shape[0]
    n = both * 2
    width = mine.shape[1] - MORE
    slots = plane * count
    facts = pl.BlockSpec((both // 2, MORE), lambda j: (0, width // MORE))
    part = pl.BlockSpec((both, STEP), lambda j: (0, j))
    one = pl.BlockSpec((both // 2, STEP), lambda j: (0, j))
    whole = pl.BlockSpec((n, slots), lambda j: (0, 0))
    return pl.pallas_call(
        select_body,
        grid=(width // STEP,),
        in_specs=[pl.BlockSpec(memory_space=pltpu.SMEM)] + [facts] * 4 + [part, part, one, one, part],
        out_specs=[pl.BlockSpec((plane, 2, count, STEP), lambda j: (0, 0, 0, j))] + [whole] * 3,
        out_shape=[jax.ShapeDtypeStruct((plane, 2, count, width), BF)]
        + [jax.ShapeDtypeStruct((n, slots), BF)] * 3,
        scratch_shapes=[pltpu.VMEM((slots, n), BF), pltpu.VMEM((slots, 1), F32)],
        compiler_params=pltpu.CompilerParams(vmem_limit_bytes=GRANT),
        cost_estimate=cost(1 << 30, 6 << 20),
    )(place, mine, up, far[0], down, mine, up, *far, down)


def forward_body(x_ref, w_ref, out_ref, projected_ref):
    hid = w_ref.shape[1] // 3
    x = x_ref[...].reshape(out_ref.shape)
    projected = jnp.dot(x, w_ref[:, : 2 * hid], preferred_element_type=F32)
    projected_ref[...] = projected
    gate_part = projected[:, :hid]
    hidden = (gate_part * jax.nn.sigmoid(gate_part) * projected[:, hid:]).astype(BF)
    for j in range(0, out_ref.shape[1], STEP):
        out = lax.dot_general(hidden, w_ref[j : j + STEP, 2 * hid :], LAST, preferred_element_type=F32)
        out_ref[:, j : j + STEP] = out.astype(BF)


def backward_body(g_ref, projected_ref, w_ref, out_ref):
    hid = w_ref.shape[1] // 3
    g = g_ref[...].reshape(out_ref.shape)
    d_hidden = jnp.dot(g, w_ref[:, 2 * hid :], preferred_element_type=F32)
    gate_part = projected_ref[:, :hid]
    sig = jax.nn.sigmoid(gate_part)
    d_gate = d_hidden * projected_ref[:, hid:] * sig * (1.0 + gate_part * (1.0 - sig))
    d_upper = d_hidden * gate_part * sig
    d_joined = jnp.concatenate([d_gate.astype(BF), d_upper.astype(BF)], axis=1)
    for j in range(0, out_ref.shape[1], STEP):
        out = lax.dot_general(d_joined, w_ref[j : j + STEP, : 2 * hid], LAST, preferred_element_type=F32)
        out_ref[:, j : j + STEP] = out.astype(BF)


def expert_specs(rows, weights, which):
    plane, _, count, width = rows.shape
    hid = weights.shape[1] // 3
    taken = pl.BlockSpec((ROWS // count, None, count, width), lambda i: (i, which, 0, 0))
    row = pl.BlockSpec((ROWS, width), lambda i: (i, 0))
    middle = pl.BlockSpec((ROWS, 2 * hid), lambda i: (i, 0))
    whole = pl.BlockSpec(weights.shape, lambda i: (0, 0), pipeline_mode=pl.Buffered(1))
    total = plane * count
    out = jax.ShapeDtypeStruct((total, width), BF)
    return (total // ROWS,), taken, row, middle, whole, out, jax.ShapeDtypeStruct((total, 2 * hid), F32)


def forward(rows, weights):
    grid, taken, row, middle, whole, out, projected = expert_specs(rows, weights, 0)
    return pl.pallas_call(
        forward_body,
        grid=grid,
        in_specs=[taken, whole],
        out_specs=[row, middle],
        out_shape=[out, projected],
        compiler_params=pltpu.CompilerParams(vmem_limit_bytes=GRANT),
        cost_estimate=cost(5 << 29, 10 << 20),
    )(rows, weights)


def backward(rows, projected, weights):
    grid, taken, row, middle, whole, out, _ = expert_specs(rows, weights, 1)
    return pl.pallas_call(
        backward_body,
        grid=grid,
        in_specs=[taken, middle, whole],
        out_specs=row,
        out_shape=out,
        compiler_params=pltpu.CompilerParams(vmem_limit_bytes=GRANT),
        cost_estimate=cost(5 << 29, 10 << 20),
    )(rows, projected, weights)


def combine_body(count, *refs):
    factors, rows, own_ref = refs[:count], refs[count][...], refs[count + 1]
    total = jnp.dot(factors[0][...], rows, preferred_element_type=F32)
    for f in factors[1:]:
        total = total + jnp.dot(f[...], rows, preferred_element_type=F32)
    m = own_ref.shape[0]
    own_ref[...] = total[:m]
    for s, ref in enumerate(refs[count + 2 :], 1):
        ref[...] = total[s * m : (s + 1) * m].astype(BF)


def combine(factors, rows):
    n, slots = factors[0].shape
    width = rows.shape[1]
    part = pl.BlockSpec((n // 4, STEP), lambda j: (0, j))
    return pl.pallas_call(
        functools.partial(combine_body, len(factors)),
        grid=(width // STEP,),
        in_specs=[pl.BlockSpec((n, slots), lambda j: (0, 0))] * len(factors)
        + [pl.BlockSpec((slots, STEP), lambda j: (0, j))],
        out_specs=[part] * 4,
        out_shape=[jax.ShapeDtypeStruct((n // 4, width), F32)]
        + [jax.ShapeDtypeStruct((n // 4, width), BF)] * 3,
        compiler_params=pltpu.CompilerParams(vmem_limit_bytes=16 << 20),
        cost_estimate=cost(1 << 28, 3 << 20),
    )(*factors, rows)


def in_plane(rows):
    return lax.all_to_all(rows, PLANE, 0, 0, tiled=True)


def local(hidden_in, cotangent, expert_ids, route_prob, swap_flags, gate_up, down_t):
    micro, tok, width = hidden_in.shape
    top = expert_ids.shape[2]
    hid = down_t.shape[2]
    nz = lax.axis_size("z")
    ny = lax.axis_size("y")
    plane = ny * lax.axis_size("x") * 2
    count = micro * nz * 2
    my_z = lax.axis_index("z")
    half = ny * lax.axis_size("x") * nz
    my_index = lax.axis_index(EXPERT)

    weights = jnp.concatenate([gate_up.reshape(-1, 2 * hid), down_t.reshape(-1, hid)], axis=1)
    weights = lax.all_gather(weights, "dp", axis=0, tiled=True)

    flag = jnp.sum(jnp.where(jnp.arange(half, dtype=jnp.int32) == my_index % half, swap_flags, 0))
    pairs = [(i, i ^ (ny // 2)) for i in range(ny)]

    high = lax.reduce_precision(route_prob, 8, 7)
    middle = lax.reduce_precision(route_prob - high, 8, 7)
    low = route_prob - high - middle
    facts = jnp.concatenate([expert_ids.astype(F32), high, middle, low], axis=2).astype(BF)
    facts = jnp.pad(facts.reshape(micro * tok, 4 * top), ((0, micro * tok), (0, MORE - 4 * top)))
    mine = jnp.concatenate([hidden_in, cotangent], axis=0).reshape(2 * micro * tok, width)
    mine = jnp.concatenate([mine, facts], axis=1)
    gate_own, down_own, mine = lax.optimization_barrier((gate_up, down_t, mine))
    other_gate = lax.ppermute(gate_own, "y", pairs)
    other_down = lax.ppermute(down_own, "y", pairs)
    up, down = along_z(mine, 1), along_z(mine, -1)
    split = micro * tok
    far = (along_z(up[:split], 1), along_z(down[split:], -1))

    rows, back, w_high, w_low = select(jnp.full((1,), my_z, jnp.int32), mine, up, far, down, plane, count)
    rows, other_gate, other_down = lax.optimization_barrier((rows, other_gate, other_down))
    rows = in_plane(rows)

    expert_out, projected = forward(rows, weights)
    back_out = in_plane(expert_out.reshape(plane, count, width)).reshape(plane * count, width)
    row_input = backward(rows, projected, weights)
    back_out, row_input = lax.optimization_barrier((back_out, row_input))
    back_grad = in_plane(row_input.reshape(plane, count, width)).reshape(plane * count, width)
    resident_gate = jnp.where(flag == 1, other_gate, gate_up)
    resident_down = jnp.where(flag == 1, other_down, down_t)

    results = []
    for factors, moved in (((w_high, w_low), back_out), ((back,), back_grad)):
        own, *others = combine(factors, moved)
        for s, part in enumerate(others, 1):
            own = own + along_z(part, -s).astype(F32)
        results.append(own.astype(BF).reshape(micro, tok, width))
    return (results[0], results[1], resident_gate, resident_down)


def solution(mesh):
    devices = mesh.devices.reshape(4, 4, 4, 4, 2)
    fine = Mesh(devices, ("dp", "y", "x", "z", "c"))
    tokens = P(None, ("dp",) + EXPERT, None)
    placed = (
        tokens,
        tokens,
        tokens,
        tokens,
        P(),
        P(EXPERT, "dp", None, None),
        P(EXPERT, "dp", None),
    )
    return jax.shard_map(
        local,
        mesh=fine,
        in_specs=placed,
        out_specs=(tokens, tokens, P(EXPERT, "dp", None, None), P(EXPERT, "dp", None)),
        check_vma=False,
    )
```

```python
import functools

import jax
import jax.numpy as jnp
from jax import lax
from jax.experimental import pallas as pl
from jax.experimental.pallas import tpu as pltpu
from jax.sharding import Mesh, PartitionSpec as P

EXPERT = ("y", "x", "z", "c")
PLANE = ("y", "x", "c")
BF = jnp.bfloat16
F32 = jnp.float32
STEP = 512
MORE = 128
ROWS = 256
GRANT = 60 << 20
LAST = (((1,), (1,)), ((), ()))


def along_z(value, shift):
    count = lax.axis_size("z")
    return lax.ppermute(value, "z", [(i, (i + shift) % count) for i in range(count)])


def cost(flops, size):
    return pl.CostEstimate(flops=flops, bytes_accessed=size, transcendentals=0)


def route_body(place_ref, f0, f1, f2, f3, pick_ref, scale_ref, back_ref, high_ref, low_ref):
    n, slots = back_ref.shape
    facts = jnp.concatenate([f[...] for f in (f0, f1, f2, f3)], axis=0).astype(F32)
    ids = facts[:, 0:8].astype(jnp.int32)
    prob = facts[:, 8:16] + facts[:, 16:24] + facts[:, 24:32]
    place = jnp.where(((ids >> 1) & 3) == place_ref[0], ((ids >> 3) << 1) + (ids & 1), -1)
    col = lax.broadcasted_iota(jnp.int32, (n, slots), 1)
    row = lax.broadcasted_iota(jnp.int32, (n, slots), 0)
    dest = col >> 4
    hit = jnp.zeros((n, slots), jnp.bool_)
    weight = jnp.zeros((n, slots), F32)
    for k in range(8):
        same = place[:, k : k + 1] == dest
        hit = hit | same
        weight = jnp.where(same, prob[:, k : k + 1], weight)
    r2 = lax.broadcasted_iota(jnp.int32, (n, n), 0)
    c2 = lax.broadcasted_iota(jnp.int32, (n, n), 1)
    below = ((c2 < r2) & ((c2 >> 4) == (r2 >> 4))).astype(F32).astype(BF)
    earlier = jnp.dot(below, hit.astype(F32).astype(BF), preferred_element_type=F32)
    block = ((row >> 5) == ((col >> 1) & 3)) & (((row >> 4) & 1) == ((col >> 3) & 1))
    pick = hit & block & (earlier == (col & 1).astype(F32))
    pick_f = pick.astype(F32)
    scaled = jnp.where(pick, weight, 0.0)
    back_ref[...] = pick_f.astype(BF)
    high = scaled.astype(BF)
    high_ref[...] = high
    low_ref[...] = (scaled - high.astype(F32)).astype(BF)
    pick_ref[...] = jnp.transpose(pick_f).astype(BF)
    scale_ref[...] = jnp.sum(jnp.transpose(scaled), axis=1, keepdims=True)


def route(place, mine, up, far, down, slots):
    tokens = mine.shape[0] // 2
    n = tokens * 4
    last = mine.shape[1] // MORE - 1
    facts = pl.BlockSpec((tokens, MORE), lambda i: (0, last))

    def whole(a, b):
        return pl.BlockSpec((a, b), lambda i: (0, 0))

    return pl.pallas_call(
        route_body,
        grid=(1,),
        in_specs=[pl.BlockSpec(memory_space=pltpu.SMEM)] + [facts] * 4,
        out_specs=[whole(slots, n), whole(slots, 1)] + [whole(n, slots)] * 3,
        out_shape=[jax.ShapeDtypeStruct((slots, n), BF), jax.ShapeDtypeStruct((slots, 1), F32)]
        + [jax.ShapeDtypeStruct((n, slots), BF)] * 3,
        compiler_params=pltpu.CompilerParams(vmem_limit_bytes=16 << 20),
        cost_estimate=cost(1 << 26, 1 << 20),
    )(place, mine, up, far, down)


def select_tokens_body(pick_ref, a0, a1, a2, a3, rows_ref):
    tokens = jnp.concatenate([a[...] for a in (a0, a1, a2, a3)], axis=0)
    rows = jnp.dot(pick_ref[...], tokens, preferred_element_type=F32)
    rows_ref[...] = rows.astype(BF).reshape(rows_ref.shape)


def select_grads_body(pick_ref, scale_ref, a0, a1, a2, a3, _, rows_ref):
    tokens = jnp.concatenate([a[...] for a in (a0, a1, a2, a3)], axis=0)
    rows = jnp.dot(pick_ref[...], tokens, preferred_element_type=F32)
    rows_ref[...] = (rows * scale_ref[...]).astype(BF).reshape(rows_ref.shape)


def select(pick, mine, up, far, down, plane, scale=None, rows=None):
    slots, n = pick.shape
    part, width = n // 4, mine.shape[1] - MORE
    which = 0 if rows is None else 1
    step = 2 * STEP
    near = pl.BlockSpec((part, step), lambda j: (which, j))
    distant = pl.BlockSpec((part, step), lambda j: (0, j))
    whole = pl.BlockSpec((slots, n), lambda j: (0, 0))
    specs = [near, near, distant, near]
    if which:
        specs = [whole, pl.BlockSpec((slots, 1), lambda j: (0, 0)), *specs, pl.BlockSpec(memory_space=pl.ANY)]
        operands = (pick, scale, mine, up, far, down, rows)
    else:
        specs = [whole, *specs]
        operands = (pick, mine, up, far, down)
    return pl.pallas_call(
        select_grads_body if which else select_tokens_body,
        grid=(width // step,),
        in_specs=specs,
        out_specs=pl.BlockSpec((plane, None, slots // plane, step), lambda j: (0, which, 0, j)),
        out_shape=jax.ShapeDtypeStruct((plane, 2, slots // plane, width), BF),
        input_output_aliases={len(operands) - 1: 0} if which else {},
        compiler_params=pltpu.CompilerParams(vmem_limit_bytes=GRANT),
        cost_estimate=cost(1 << 29, 3 << 20),
    )(*operands)


def forward_body(rows_hbm, weights_hbm, out_hbm, x_ref, w_ref, out_ref, came, went):
    plane, _, count, width = rows_hbm.shape
    hid = w_ref.shape[2] // 3
    steps = width // STEP

    def taken(k):
        columns = pl.ds(k * STEP, STEP)
        return (
            pltpu.make_async_copy(rows_hbm.at[:, 0, :, columns], x_ref.at[k], came.at[2 * k]),
            pltpu.make_async_copy(weights_hbm.at[columns], w_ref.at[k], came.at[2 * k + 1]),
        )

    def given(k):
        return pltpu.make_async_copy(out_ref.at[k], out_hbm.at[:, pl.ds(k * STEP, STEP)], went.at[k])

    for k in range(steps):
        for copy in taken(k):
            copy.start()
    projected = None
    for k in range(steps):
        for copy in taken(k):
            copy.wait()
        x = x_ref[k].reshape(plane * count, STEP)
        term = jnp.dot(x, w_ref[k, :, : 2 * hid], preferred_element_type=F32)
        projected = term if projected is None else projected + term
    gate_part = projected[:, :hid]
    hidden = (gate_part * jax.nn.sigmoid(gate_part) * projected[:, hid:]).astype(BF)
    for k in range(steps):
        out = lax.dot_general(hidden, w_ref[k, :, 2 * hid :], LAST, preferred_element_type=F32)
        out_ref[k] = out.astype(BF)
        given(k).start()
    for k in range(steps):
        given(k).wait()


def forward(rows, weights):
    plane, _, count, width = rows.shape
    total, steps = plane * count, width // STEP
    anywhere = pl.BlockSpec(memory_space=pl.ANY)
    return pl.pallas_call(
        forward_body,
        in_specs=[anywhere, anywhere],
        out_specs=anywhere,
        out_shape=jax.ShapeDtypeStruct((total, width), BF),
        scratch_shapes=[
            pltpu.VMEM((steps, plane, count, STEP), BF),
            pltpu.VMEM((steps, STEP, weights.shape[1]), BF),
            pltpu.VMEM((steps, total, STEP), BF),
            pltpu.SemaphoreType.DMA((2 * steps,)),
            pltpu.SemaphoreType.DMA((steps,)),
        ],
        compiler_params=pltpu.CompilerParams(vmem_limit_bytes=GRANT),
        cost_estimate=cost(5 << 29, 10 << 20),
    )(rows, weights)


def backward_body(x_ref, g_ref, w_ref, out_ref):
    hid = w_ref.shape[1] // 3
    x = x_ref[...].reshape(out_ref.shape)
    g = g_ref[...].reshape(out_ref.shape)
    projected = jnp.dot(x, w_ref[:, : 2 * hid], preferred_element_type=F32)
    d_hidden = jnp.dot(g, w_ref[:, 2 * hid :], preferred_element_type=F32)
    gate_part = projected[:, :hid]
    sig = jax.nn.sigmoid(gate_part)
    d_gate = d_hidden * projected[:, hid:] * sig * (1.0 + gate_part * (1.0 - sig))
    d_upper = d_hidden * gate_part * sig
    d_joined = jnp.concatenate([d_gate.astype(BF), d_upper.astype(BF)], axis=1)
    for j in range(0, out_ref.shape[1], STEP):
        out = lax.dot_general(d_joined, w_ref[j : j + STEP, : 2 * hid], LAST, preferred_element_type=F32)
        out_ref[:, j : j + STEP] = out.astype(BF)


def backward(rows, weights):
    plane, _, count, width = rows.shape
    total = plane * count

    def taken(which):
        return pl.BlockSpec((ROWS // count, None, count, width), lambda i: (i, which, 0, 0))

    return pl.pallas_call(
        backward_body,
        grid=(total // ROWS,),
        in_specs=[
            taken(0),
            taken(1),
            pl.BlockSpec(weights.shape, lambda i: (0, 0), pipeline_mode=pl.Buffered(1)),
        ],
        out_specs=pl.BlockSpec((ROWS, width), lambda i: (i, 0)),
        out_shape=jax.ShapeDtypeStruct((total, width), BF),
        compiler_params=pltpu.CompilerParams(vmem_limit_bytes=GRANT),
        cost_estimate=cost(7 << 29, 10 << 20),
    )(rows, rows, weights)


def combine_body(count, *refs):
    factors, rows, own_ref = refs[:count], refs[count][...], refs[count + 1]
    total = jnp.dot(factors[0][...], rows, preferred_element_type=F32)
    for f in factors[1:]:
        total = total + jnp.dot(f[...], rows, preferred_element_type=F32)
    m = own_ref.shape[0]
    own_ref[...] = total[:m]
    for s, ref in enumerate(refs[count + 2 :], 1):
        ref[...] = total[s * m : (s + 1) * m].astype(BF)


def combine(factors, rows):
    n, slots = factors[0].shape
    width = rows.shape[1]
    part = pl.BlockSpec((n // 4, STEP), lambda j: (0, j))
    return pl.pallas_call(
        functools.partial(combine_body, len(factors)),
        grid=(width // STEP,),
        in_specs=[pl.BlockSpec((n, slots), lambda j: (0, 0))] * len(factors)
        + [pl.BlockSpec((slots, STEP), lambda j: (0, j))],
        out_specs=[part] * 4,
        out_shape=[jax.ShapeDtypeStruct((n // 4, width), F32)]
        + [jax.ShapeDtypeStruct((n // 4, width), BF)] * 3,
        compiler_params=pltpu.CompilerParams(vmem_limit_bytes=16 << 20),
        cost_estimate=cost(1 << 28, 3 << 20),
    )(*factors, rows)


def in_plane(rows):
    return lax.all_to_all(rows, PLANE, 0, 0, tiled=True)


def local(hidden_in, cotangent, expert_ids, route_prob, swap_flags, gate_up, down_t):
    micro, tok, width = hidden_in.shape
    top = expert_ids.shape[2]
    hid = down_t.shape[2]
    nz = lax.axis_size("z")
    ny = lax.axis_size("y")
    plane = ny * lax.axis_size("x") * 2
    count = micro * nz * 2
    my_z = lax.axis_index("z")
    half = ny * lax.axis_size("x") * nz
    my_index = lax.axis_index(EXPERT)

    weights = jnp.concatenate([gate_up.reshape(-1, 2 * hid), down_t.reshape(-1, hid)], axis=1)
    weights = lax.all_gather(weights, "dp", axis=0, tiled=True)

    flag = jnp.sum(jnp.where(jnp.arange(half, dtype=jnp.int32) == my_index % half, swap_flags, 0))
    pairs = [(i, i ^ (ny // 2)) for i in range(ny)]

    high = lax.reduce_precision(route_prob, 8, 7)
    middle = lax.reduce_precision(route_prob - high, 8, 7)
    low = route_prob - high - middle
    facts = jnp.concatenate([expert_ids.astype(F32), high, middle, low], axis=2).astype(BF)
    facts = jnp.pad(facts.reshape(micro * tok, 4 * top), ((0, micro * tok), (0, MORE - 4 * top)))
    mine = jnp.concatenate([hidden_in, cotangent], axis=0).reshape(2 * micro * tok, width)
    mine = jnp.concatenate([mine, facts], axis=1)
    gate_own, down_own, mine = lax.optimization_barrier((gate_up, down_t, mine))
    other_gate = lax.ppermute(gate_own, "y", pairs)
    other_down = lax.ppermute(down_own, "y", pairs)
    up, down = along_z(mine, 1), along_z(mine, -1)
    split = micro * tok
    far = (along_z(down[:split], -1), along_z(up[split:], 1))

    place = jnp.full((1,), my_z, jnp.int32)
    pick, scale, back, w_high, w_low = route(place, mine, up, far[0], down, plane * count)
    rows = select(pick, mine, up, far[0], down, plane)
    rows = select(pick, mine, up, far[1], down, plane, scale, rows)
    rows, other_gate, other_down = lax.optimization_barrier((rows, other_gate, other_down))
    rows = in_plane(rows)

    expert_out = forward(rows, weights)
    back_out = in_plane(expert_out.reshape(plane, count, width)).reshape(plane * count, width)
    row_input = backward(rows, weights)
    back_out, row_input = lax.optimization_barrier((back_out, row_input))
    back_grad = in_plane(row_input.reshape(plane, count, width)).reshape(plane * count, width)
    resident_gate = jnp.where(flag == 1, other_gate, gate_up)
    resident_down = jnp.where(flag == 1, other_down, down_t)

    results = []
    for factors, moved in (((w_high, w_low), back_out), ((back,), back_grad)):
        own, *others = combine(factors, moved)
        for s, part in enumerate(others, 1):
            own = own + along_z(part, -s).astype(F32)
        results.append(own.astype(BF).reshape(micro, tok, width))
    return (results[0], results[1], resident_gate, resident_down)


def solution(mesh):
    devices = mesh.devices.reshape(4, 4, 4, 4, 2)
    fine = Mesh(devices, ("dp", "y", "x", "z", "c"))
    tokens = P(None, ("dp",) + EXPERT, None)
    placed = (
        tokens,
        tokens,
        tokens,
        tokens,
        P(),
        P(EXPERT, "dp", None, None),
        P(EXPERT, "dp", None),
    )
    return jax.shard_map(
        local,
        mesh=fine,
        in_specs=placed,
        out_specs=(tokens, tokens, P(EXPERT, "dp", None, None), P(EXPERT, "dp", None)),
        check_vma=False,
    )
```

```python
import functools

import jax
import jax.numpy as jnp
from jax import lax
from jax.experimental import pallas as pl
from jax.experimental.pallas import tpu as pltpu
from jax.sharding import Mesh, PartitionSpec as P

EXPERT = ("y", "x", "z", "c")
PLANE = ("y", "x", "c")
BF = jnp.bfloat16
F32 = jnp.float32
STEP = 512
MORE = 128
ROWS = 256
GRANT = 60 << 20
LAST = (((1,), (1,)), ((), ()))


def along_z(value, shift):
    count = lax.axis_size("z")
    return lax.ppermute(value, "z", [(i, (i + shift) % count) for i in range(count)])


def cost(flops, size):
    return pl.CostEstimate(flops=flops, bytes_accessed=size, transcendentals=0)


def route_body(place_ref, f0, f1, f2, f3, pick_ref, scale_ref, back_ref, high_ref, low_ref):
    n, slots = back_ref.shape
    facts = jnp.concatenate([f[...] for f in (f0, f1, f2, f3)], axis=0).astype(F32)
    ids = facts[:, 0:8].astype(jnp.int32)
    prob = facts[:, 8:16] + facts[:, 16:24] + facts[:, 24:32]
    place = jnp.where(((ids >> 1) & 3) == place_ref[0], ((ids >> 3) << 1) + (ids & 1), -1)
    col = lax.broadcasted_iota(jnp.int32, (n, slots), 1)
    row = lax.broadcasted_iota(jnp.int32, (n, slots), 0)
    dest = col >> 4
    hit = jnp.zeros((n, slots), jnp.bool_)
    weight = jnp.zeros((n, slots), F32)
    for k in range(8):
        same = place[:, k : k + 1] == dest
        hit = hit | same
        weight = jnp.where(same, prob[:, k : k + 1], weight)
    r2 = lax.broadcasted_iota(jnp.int32, (n, n), 0)
    c2 = lax.broadcasted_iota(jnp.int32, (n, n), 1)
    below = ((c2 < r2) & ((c2 >> 4) == (r2 >> 4))).astype(F32).astype(BF)
    earlier = jnp.dot(below, hit.astype(F32).astype(BF), preferred_element_type=F32)
    block = ((row >> 5) == ((col >> 1) & 3)) & (((row >> 4) & 1) == ((col >> 3) & 1))
    pick = hit & block & (earlier == (col & 1).astype(F32))
    pick_f = pick.astype(F32)
    scaled = jnp.where(pick, weight, 0.0)
    back_ref[...] = pick_f.astype(BF)
    high = scaled.astype(BF)
    high_ref[...] = high
    low_ref[...] = (scaled - high.astype(F32)).astype(BF)
    pick_ref[...] = jnp.transpose(pick_f).astype(BF)
    scale_ref[...] = jnp.sum(jnp.transpose(scaled), axis=1, keepdims=True)


def route(place, mine, up, far, down, slots):
    tokens = mine.shape[0] // 2
    n = tokens * 4
    last = mine.shape[1] // MORE - 1
    facts = pl.BlockSpec((tokens, MORE), lambda i: (0, last))

    def whole(a, b):
        return pl.BlockSpec((a, b), lambda i: (0, 0))

    return pl.pallas_call(
        route_body,
        grid=(1,),
        in_specs=[pl.BlockSpec(memory_space=pltpu.SMEM)] + [facts] * 4,
        out_specs=[whole(slots, n), whole(slots, 1)] + [whole(n, slots)] * 3,
        out_shape=[jax.ShapeDtypeStruct((slots, n), BF), jax.ShapeDtypeStruct((slots, 1), F32)]
        + [jax.ShapeDtypeStruct((n, slots), BF)] * 3,
        compiler_params=pltpu.CompilerParams(vmem_limit_bytes=16 << 20),
        cost_estimate=cost(1 << 26, 1 << 20),
    )(place, mine, up, far, down)


def select_tokens_body(pick_ref, a0, a1, a2, a3, rows_ref):
    tokens = jnp.concatenate([a[...] for a in (a0, a1, a2, a3)], axis=0)
    rows = jnp.dot(pick_ref[...], tokens, preferred_element_type=F32)
    rows_ref[...] = rows.astype(BF).reshape(rows_ref.shape)


def select_grads_body(pick_ref, scale_ref, a0, a1, a2, a3, _, rows_ref):
    tokens = jnp.concatenate([a[...] for a in (a0, a1, a2, a3)], axis=0)
    rows = jnp.dot(pick_ref[...], tokens, preferred_element_type=F32)
    rows_ref[...] = (rows * scale_ref[...]).astype(BF).reshape(rows_ref.shape)


def select(pick, mine, up, far, down, plane, scale=None, rows=None):
    slots, n = pick.shape
    part, width = n // 4, mine.shape[1] - MORE
    which = 0 if rows is None else 1
    step = 2 * STEP
    near = pl.BlockSpec((part, step), lambda j: (which, j))
    distant = pl.BlockSpec((part, step), lambda j: (0, j))
    whole = pl.BlockSpec((slots, n), lambda j: (0, 0))
    specs = [near, near, distant, near]
    if which:
        specs = [whole, pl.BlockSpec((slots, 1), lambda j: (0, 0)), *specs, pl.BlockSpec(memory_space=pl.ANY)]
        operands = (pick, scale, mine, up, far, down, rows)
    else:
        specs = [whole, *specs]
        operands = (pick, mine, up, far, down)
    return pl.pallas_call(
        select_grads_body if which else select_tokens_body,
        grid=(width // step,),
        in_specs=specs,
        out_specs=pl.BlockSpec((plane, None, slots // plane, step), lambda j: (0, which, 0, j)),
        out_shape=jax.ShapeDtypeStruct((plane, 2, slots // plane, width), BF),
        input_output_aliases={len(operands) - 1: 0} if which else {},
        compiler_params=pltpu.CompilerParams(vmem_limit_bytes=GRANT),
        cost_estimate=cost(1 << 29, 3 << 20),
    )(*operands)


def forward_body(rows_hbm, weights_hbm, out_hbm, x_ref, w_ref, out_ref, came, went):
    plane, _, count, width = rows_hbm.shape
    hid = w_ref.shape[2] // 3
    steps = width // STEP

    def taken(k):
        columns = pl.ds(k * STEP, STEP)
        return (
            pltpu.make_async_copy(rows_hbm.at[:, 0, :, columns], x_ref.at[k], came.at[2 * k]),
            pltpu.make_async_copy(weights_hbm.at[columns], w_ref.at[k], came.at[2 * k + 1]),
        )

    def given(k):
        return pltpu.make_async_copy(out_ref.at[k], out_hbm.at[:, pl.ds(k * STEP, STEP)], went.at[k])

    for k in range(steps):
        for copy in taken(k):
            copy.start()
    projected = None
    for k in range(steps):
        for copy in taken(k):
            copy.wait()
        x = x_ref[k].reshape(plane * count, STEP)
        term = jnp.dot(x, w_ref[k, :, : 2 * hid], preferred_element_type=F32)
        projected = term if projected is None else projected + term
    gate_part = projected[:, :hid]
    hidden = (gate_part * jax.nn.sigmoid(gate_part) * projected[:, hid:]).astype(BF)
    for k in range(steps):
        out = lax.dot_general(hidden, w_ref[k, :, 2 * hid :], LAST, preferred_element_type=F32)
        out_ref[k] = out.astype(BF)
        given(k).start()
    for k in range(steps):
        given(k).wait()


def forward(rows, weights):
    plane, _, count, width = rows.shape
    total, steps = plane * count, width // STEP
    anywhere = pl.BlockSpec(memory_space=pl.ANY)
    return pl.pallas_call(
        forward_body,
        in_specs=[anywhere, anywhere],
        out_specs=anywhere,
        out_shape=jax.ShapeDtypeStruct((total, width), BF),
        scratch_shapes=[
            pltpu.VMEM((steps, plane, count, STEP), BF),
            pltpu.VMEM((steps, STEP, weights.shape[1]), BF),
            pltpu.VMEM((steps, total, STEP), BF),
            pltpu.SemaphoreType.DMA((2 * steps,)),
            pltpu.SemaphoreType.DMA((steps,)),
        ],
        compiler_params=pltpu.CompilerParams(vmem_limit_bytes=GRANT),
        cost_estimate=cost(5 << 29, 10 << 20),
    )(rows, weights)


def backward_body(x_ref, g_ref, w_ref, out_ref):
    hid = w_ref.shape[1] // 3
    x = x_ref[...].reshape(out_ref.shape)
    g = g_ref[...].reshape(out_ref.shape)
    projected = jnp.dot(x, w_ref[:, : 2 * hid], preferred_element_type=F32)
    d_hidden = jnp.dot(g, w_ref[:, 2 * hid :], preferred_element_type=F32)
    gate_part = projected[:, :hid]
    sig = jax.nn.sigmoid(gate_part)
    d_gate = d_hidden * projected[:, hid:] * sig * (1.0 + gate_part * (1.0 - sig))
    d_upper = d_hidden * gate_part * sig
    d_joined = jnp.concatenate([d_gate.astype(BF), d_upper.astype(BF)], axis=1)
    for j in range(0, out_ref.shape[1], STEP):
        out = lax.dot_general(d_joined, w_ref[j : j + STEP, : 2 * hid], LAST, preferred_element_type=F32)
        out_ref[:, j : j + STEP] = out.astype(BF)


def backward(rows, weights):
    plane, _, count, width = rows.shape
    total = plane * count

    def taken(which):
        return pl.BlockSpec((ROWS // count, None, count, width), lambda i: (i, which, 0, 0))

    return pl.pallas_call(
        backward_body,
        grid=(total // ROWS,),
        in_specs=[
            taken(0),
            taken(1),
            pl.BlockSpec(weights.shape, lambda i: (0, 0), pipeline_mode=pl.Buffered(1)),
        ],
        out_specs=pl.BlockSpec((ROWS, width), lambda i: (i, 0)),
        out_shape=jax.ShapeDtypeStruct((total, width), BF),
        compiler_params=pltpu.CompilerParams(vmem_limit_bytes=GRANT),
        cost_estimate=cost(7 << 29, 10 << 20),
    )(rows, rows, weights)


def combine_body(count, *refs):
    factors, rows, own_ref = refs[:count], refs[count][...], refs[count + 1]
    total = jnp.dot(factors[0][...], rows, preferred_element_type=F32)
    for f in factors[1:]:
        total = total + jnp.dot(f[...], rows, preferred_element_type=F32)
    m = own_ref.shape[0]
    own_ref[...] = total[:m]
    for s, ref in enumerate(refs[count + 2 :], 1):
        ref[...] = total[s * m : (s + 1) * m].astype(BF)


def combine(factors, rows):
    n, slots = factors[0].shape
    width = rows.shape[1]
    part = pl.BlockSpec((n // 4, STEP), lambda j: (0, j))
    return pl.pallas_call(
        functools.partial(combine_body, len(factors)),
        grid=(width // STEP,),
        in_specs=[pl.BlockSpec((n, slots), lambda j: (0, 0))] * len(factors)
        + [pl.BlockSpec((slots, STEP), lambda j: (0, j))],
        out_specs=[part] * 4,
        out_shape=[jax.ShapeDtypeStruct((n // 4, width), F32)]
        + [jax.ShapeDtypeStruct((n // 4, width), BF)] * 3,
        compiler_params=pltpu.CompilerParams(vmem_limit_bytes=16 << 20),
        cost_estimate=cost(1 << 28, 3 << 20),
    )(*factors, rows)


def in_plane(rows):
    return lax.all_to_all(rows, PLANE, 0, 0, tiled=True)


def local(hidden_in, cotangent, expert_ids, route_prob, swap_flags, gate_up, down_t):
    micro, tok, width = hidden_in.shape
    top = expert_ids.shape[2]
    hid = down_t.shape[2]
    nz = lax.axis_size("z")
    ny = lax.axis_size("y")
    plane = ny * lax.axis_size("x") * 2
    count = micro * nz * 2
    my_z = lax.axis_index("z")
    half = ny * lax.axis_size("x") * nz
    my_index = lax.axis_index(EXPERT)

    weights = jnp.concatenate([gate_up.reshape(-1, 2 * hid), down_t.reshape(-1, hid)], axis=1)
    weights = lax.all_gather(weights, "dp", axis=0, tiled=True)

    flag = jnp.sum(jnp.where(jnp.arange(half, dtype=jnp.int32) == my_index % half, swap_flags, 0))
    pairs = [(i, i ^ (ny // 2)) for i in range(ny)]

    high = lax.reduce_precision(route_prob, 8, 7)
    middle = lax.reduce_precision(route_prob - high, 8, 7)
    low = route_prob - high - middle
    facts = jnp.concatenate([expert_ids.astype(F32), high, middle, low], axis=2).astype(BF)
    facts = jnp.pad(facts.reshape(micro * tok, 4 * top), ((0, micro * tok), (0, MORE - 4 * top)))
    mine = jnp.concatenate([hidden_in, cotangent], axis=0).reshape(2 * micro * tok, width)
    mine = jnp.concatenate([mine, facts], axis=1)
    gate_own, down_own, mine = lax.optimization_barrier((gate_up, down_t, mine))
    other_gate = [lax.ppermute(part, "y", pairs) for part in jnp.split(gate_own, 2, axis=1)]
    other_down = lax.ppermute(down_own, "y", pairs)
    up, down = along_z(mine, 1), along_z(mine, -1)
    split = micro * tok
    far = (along_z(down[:split], -1), along_z(up[split:], 1))

    place = jnp.full((1,), my_z, jnp.int32)
    pick, scale, back, w_high, w_low = route(place, mine, up, far[0], down, plane * count)
    rows = select(pick, mine, up, far[0], down, plane)
    rows = select(pick, mine, up, far[1], down, plane, scale, rows)
    rows, other_gate, other_down = lax.optimization_barrier((rows, other_gate, other_down))
    other_gate = jnp.concatenate(other_gate, axis=1)
    rows = in_plane(rows)

    expert_out = forward(rows, weights)
    back_out = in_plane(expert_out.reshape(plane, count, width)).reshape(plane * count, width)
    row_input = backward(rows, weights)
    back_out, row_input = lax.optimization_barrier((back_out, row_input))
    back_grad = in_plane(row_input.reshape(plane, count, width)).reshape(plane * count, width)
    resident_gate = jnp.where(flag == 1, other_gate, gate_up)
    resident_down = jnp.where(flag == 1, other_down, down_t)

    results = []
    for factors, moved in (((w_high, w_low), back_out), ((back,), back_grad)):
        own, *others = combine(factors, moved)
        for s, part in enumerate(others, 1):
            own = own + along_z(part, -s).astype(F32)
        results.append(own.astype(BF).reshape(micro, tok, width))
    return (results[0], results[1], resident_gate, resident_down)


def solution(mesh):
    devices = mesh.devices.reshape(4, 4, 4, 4, 2)
    fine = Mesh(devices, ("dp", "y", "x", "z", "c"))
    tokens = P(None, ("dp",) + EXPERT, None)
    placed = (
        tokens,
        tokens,
        tokens,
        tokens,
        P(),
        P(EXPERT, "dp", None, None),
        P(EXPERT, "dp", None),
    )
    return jax.shard_map(
        local,
        mesh=fine,
        in_specs=placed,
        out_specs=(tokens, tokens, P(EXPERT, "dp", None, None), P(EXPERT, "dp", None)),
        check_vma=False,
    )
```

```python
import functools

import jax
import jax.numpy as jnp
from jax import lax
from jax.experimental import pallas as pl
from jax.experimental.pallas import tpu as pltpu
from jax.sharding import Mesh, PartitionSpec as P

EXPERT = ("y", "x", "z", "c")
PLANE = ("y", "x", "c")
BF = jnp.bfloat16
F32 = jnp.float32
STEP = 512
MORE = 128
ROWS = 256
GRANT = 60 << 20
LAST = (((1,), (1,)), ((), ()))


def along_z(value, shift):
    count = lax.axis_size("z")
    return lax.ppermute(value, "z", [(i, (i + shift) % count) for i in range(count)])


def cost(flops, size):
    return pl.CostEstimate(flops=flops, bytes_accessed=size, transcendentals=0)


def route_body(place_ref, f0, f1, f2, f3, pick_ref, scale_ref, back_ref, high_ref, low_ref):
    n, slots = back_ref.shape
    facts = jnp.concatenate([f[...] for f in (f0, f1, f2, f3)], axis=0).astype(F32)
    ids = facts[:, 0:8].astype(jnp.int32)
    prob = facts[:, 8:16] + facts[:, 16:24] + facts[:, 24:32]
    place = jnp.where(((ids >> 1) & 3) == place_ref[0], ((ids >> 3) << 1) + (ids & 1), -1)
    col = lax.broadcasted_iota(jnp.int32, (n, slots), 1)
    row = lax.broadcasted_iota(jnp.int32, (n, slots), 0)
    dest = col >> 4
    hit = jnp.zeros((n, slots), jnp.bool_)
    weight = jnp.zeros((n, slots), F32)
    for k in range(8):
        same = place[:, k : k + 1] == dest
        hit = hit | same
        weight = jnp.where(same, prob[:, k : k + 1], weight)
    r2 = lax.broadcasted_iota(jnp.int32, (n, n), 0)
    c2 = lax.broadcasted_iota(jnp.int32, (n, n), 1)
    below = ((c2 < r2) & ((c2 >> 4) == (r2 >> 4))).astype(F32).astype(BF)
    earlier = jnp.dot(below, hit.astype(F32).astype(BF), preferred_element_type=F32)
    block = ((row >> 5) == ((col >> 1) & 3)) & (((row >> 4) & 1) == ((col >> 3) & 1))
    pick = hit & block & (earlier == (col & 1).astype(F32))
    pick_f = pick.astype(F32)
    scaled = jnp.where(pick, weight, 0.0)
    back_ref[...] = pick_f.astype(BF)
    high = scaled.astype(BF)
    high_ref[...] = high
    low_ref[...] = (scaled - high.astype(F32)).astype(BF)
    pick_ref[...] = jnp.transpose(pick_f).astype(BF)
    scale_ref[...] = jnp.sum(jnp.transpose(scaled), axis=1, keepdims=True)


def route(place, mine, up, far, down, slots):
    tokens = mine.shape[0] // 2
    n = tokens * 4
    last = mine.shape[1] // MORE - 1
    facts = pl.BlockSpec((tokens, MORE), lambda i: (0, last))

    def whole(a, b):
        return pl.BlockSpec((a, b), lambda i: (0, 0))

    return pl.pallas_call(
        route_body,
        grid=(1,),
        in_specs=[pl.BlockSpec(memory_space=pltpu.SMEM)] + [facts] * 4,
        out_specs=[whole(slots, n), whole(slots, 1)] + [whole(n, slots)] * 3,
        out_shape=[jax.ShapeDtypeStruct((slots, n), BF), jax.ShapeDtypeStruct((slots, 1), F32)]
        + [jax.ShapeDtypeStruct((n, slots), BF)] * 3,
        compiler_params=pltpu.CompilerParams(vmem_limit_bytes=16 << 20),
        cost_estimate=cost(1 << 26, 1 << 20),
    )(place, mine, up, far, down)


def select_tokens_body(pick_ref, a0, a1, a2, a3, rows_ref):
    tokens = jnp.concatenate([a[...] for a in (a0, a1, a2, a3)], axis=0)
    rows = jnp.dot(pick_ref[...], tokens, preferred_element_type=F32)
    rows_ref[...] = rows.astype(BF).reshape(rows_ref.shape)


def select_grads_body(pick_ref, scale_ref, a0, a1, a2, a3, _, rows_ref):
    tokens = jnp.concatenate([a[...] for a in (a0, a1, a2, a3)], axis=0)
    rows = jnp.dot(pick_ref[...], tokens, preferred_element_type=F32)
    rows_ref[...] = (rows * scale_ref[...]).astype(BF).reshape(rows_ref.shape)


def select(pick, mine, up, far, down, plane, scale=None, rows=None):
    slots, n = pick.shape
    part, width = n // 4, mine.shape[1] - MORE
    which = 0 if rows is None else 1
    step = 2 * STEP
    near = pl.BlockSpec((part, step), lambda j: (which, j))
    distant = pl.BlockSpec((part, step), lambda j: (0, j))
    whole = pl.BlockSpec((slots, n), lambda j: (0, 0))
    specs = [near, near, distant, near]
    if which:
        specs = [whole, pl.BlockSpec((slots, 1), lambda j: (0, 0)), *specs, pl.BlockSpec(memory_space=pl.ANY)]
        operands = (pick, scale, mine, up, far, down, rows)
    else:
        specs = [whole, *specs]
        operands = (pick, mine, up, far, down)
    return pl.pallas_call(
        select_grads_body if which else select_tokens_body,
        grid=(width // step,),
        in_specs=specs,
        out_specs=pl.BlockSpec((plane, None, slots // plane, step), lambda j: (0, which, 0, j)),
        out_shape=jax.ShapeDtypeStruct((plane, 2, slots // plane, width), BF),
        input_output_aliases={len(operands) - 1: 0} if which else {},
        compiler_params=pltpu.CompilerParams(vmem_limit_bytes=GRANT),
        cost_estimate=cost(1 << 29, 3 << 20),
    )(*operands)


def forward_body(rows_hbm, weights_hbm, out_hbm, x_ref, w_ref, out_ref, came, went):
    plane, _, count, width = rows_hbm.shape
    hid = w_ref.shape[2] // 3
    steps = width // STEP

    def taken(k):
        columns = pl.ds(k * STEP, STEP)
        return (
            pltpu.make_async_copy(rows_hbm.at[:, 0, :, columns], x_ref.at[k], came.at[2 * k]),
            pltpu.make_async_copy(weights_hbm.at[columns], w_ref.at[k], came.at[2 * k + 1]),
        )

    def given(k):
        return pltpu.make_async_copy(out_ref.at[k], out_hbm.at[:, pl.ds(k * STEP, STEP)], went.at[k])

    for k in range(steps):
        for copy in taken(k):
            copy.start()
    projected = None
    for k in range(steps):
        for copy in taken(k):
            copy.wait()
        x = x_ref[k].reshape(plane * count, STEP)
        term = jnp.dot(x, w_ref[k, :, : 2 * hid], preferred_element_type=F32)
        projected = term if projected is None else projected + term
    gate_part = projected[:, :hid]
    hidden = (gate_part * jax.nn.sigmoid(gate_part) * projected[:, hid:]).astype(BF)
    for k in range(steps):
        out = lax.dot_general(hidden, w_ref[k, :, 2 * hid :], LAST, preferred_element_type=F32)
        out_ref[k] = out.astype(BF)
        given(k).start()
    for k in range(steps):
        given(k).wait()


def forward(rows, weights):
    plane, _, count, width = rows.shape
    total, steps = plane * count, width // STEP
    anywhere = pl.BlockSpec(memory_space=pl.ANY)
    return pl.pallas_call(
        forward_body,
        in_specs=[anywhere, anywhere],
        out_specs=anywhere,
        out_shape=jax.ShapeDtypeStruct((total, width), BF),
        scratch_shapes=[
            pltpu.VMEM((steps, plane, count, STEP), BF),
            pltpu.VMEM((steps, STEP, weights.shape[1]), BF),
            pltpu.VMEM((steps, total, STEP), BF),
            pltpu.SemaphoreType.DMA((2 * steps,)),
            pltpu.SemaphoreType.DMA((steps,)),
        ],
        compiler_params=pltpu.CompilerParams(vmem_limit_bytes=GRANT),
        cost_estimate=cost(5 << 29, 10 << 20),
    )(rows, weights)


def backward_body(x_ref, g_ref, w_ref, out_ref):
    hid = w_ref.shape[1] // 3
    x = x_ref[...].reshape(out_ref.shape)
    g = g_ref[...].reshape(out_ref.shape)
    projected = jnp.dot(x, w_ref[:, : 2 * hid], preferred_element_type=F32)
    d_hidden = jnp.dot(g, w_ref[:, 2 * hid :], preferred_element_type=F32)
    gate_part = projected[:, :hid]
    sig = jax.nn.sigmoid(gate_part)
    d_gate = d_hidden * projected[:, hid:] * sig * (1.0 + gate_part * (1.0 - sig))
    d_upper = d_hidden * gate_part * sig
    d_joined = jnp.concatenate([d_gate.astype(BF), d_upper.astype(BF)], axis=1)
    for j in range(0, out_ref.shape[1], STEP):
        out = lax.dot_general(d_joined, w_ref[j : j + STEP, : 2 * hid], LAST, preferred_element_type=F32)
        out_ref[:, j : j + STEP] = out.astype(BF)


def backward(rows, weights):
    plane, _, count, width = rows.shape
    total = plane * count

    def taken(which):
        return pl.BlockSpec((ROWS // count, None, count, width), lambda i: (i, which, 0, 0))

    return pl.pallas_call(
        backward_body,
        grid=(total // ROWS,),
        in_specs=[
            taken(0),
            taken(1),
            pl.BlockSpec(weights.shape, lambda i: (0, 0), pipeline_mode=pl.Buffered(1)),
        ],
        out_specs=pl.BlockSpec((ROWS, width), lambda i: (i, 0)),
        out_shape=jax.ShapeDtypeStruct((total, width), BF),
        compiler_params=pltpu.CompilerParams(vmem_limit_bytes=GRANT),
        cost_estimate=cost(7 << 29, 10 << 20),
    )(rows, rows, weights)


def combine_body(count, *refs):
    factors, rows, own_ref = refs[:count], refs[count][...], refs[count + 1]
    total = jnp.dot(factors[0][...], rows, preferred_element_type=F32)
    for f in factors[1:]:
        total = total + jnp.dot(f[...], rows, preferred_element_type=F32)
    m = own_ref.shape[0]
    own_ref[...] = total[:m]
    for s, ref in enumerate(refs[count + 2 :], 1):
        ref[...] = total[s * m : (s + 1) * m].astype(BF)


def combine(factors, rows):
    n, slots = factors[0].shape
    width = rows.shape[1]
    part = pl.BlockSpec((n // 4, STEP), lambda j: (0, j))
    return pl.pallas_call(
        functools.partial(combine_body, len(factors)),
        grid=(width // STEP,),
        in_specs=[pl.BlockSpec((n, slots), lambda j: (0, 0))] * len(factors)
        + [pl.BlockSpec((slots, STEP), lambda j: (0, j))],
        out_specs=[part] * 4,
        out_shape=[jax.ShapeDtypeStruct((n // 4, width), F32)]
        + [jax.ShapeDtypeStruct((n // 4, width), BF)] * 3,
        compiler_params=pltpu.CompilerParams(vmem_limit_bytes=16 << 20),
        cost_estimate=cost(1 << 28, 3 << 20),
    )(*factors, rows)


def in_plane(rows):
    return lax.all_to_all(rows, PLANE, 0, 0, tiled=True)


def local(hidden_in, cotangent, expert_ids, route_prob, swap_flags, gate_up, down_t):
    micro, tok, width = hidden_in.shape
    top = expert_ids.shape[2]
    hid = down_t.shape[2]
    nz = lax.axis_size("z")
    ny = lax.axis_size("y")
    plane = ny * lax.axis_size("x") * 2
    count = micro * nz * 2
    my_z = lax.axis_index("z")
    half = ny * lax.axis_size("x") * nz
    my_index = lax.axis_index(EXPERT)

    weights = jnp.concatenate([gate_up.reshape(-1, 2 * hid), down_t.reshape(-1, hid)], axis=1)
    weights = lax.all_gather(weights, "dp", axis=0, tiled=True)

    flag = jnp.sum(jnp.where(jnp.arange(half, dtype=jnp.int32) == my_index % half, swap_flags, 0))
    pairs = [(i, i ^ (ny // 2)) for i in range(ny)]

    high = lax.reduce_precision(route_prob, 8, 7)
    middle = lax.reduce_precision(route_prob - high, 8, 7)
    low = route_prob - high - middle
    facts = jnp.concatenate([expert_ids.astype(F32), high, middle, low], axis=2).astype(BF)
    facts = jnp.pad(facts.reshape(micro * tok, 4 * top), ((0, micro * tok), (0, MORE - 4 * top)))
    mine = jnp.concatenate([hidden_in, cotangent], axis=0).reshape(2 * micro * tok, width)
    mine = jnp.concatenate([mine, facts], axis=1)
    gate_own, down_own, mine = lax.optimization_barrier((gate_up, down_t, mine))
    other_gate = [lax.ppermute(part, "y", pairs) for part in jnp.split(gate_own, 2, axis=1)]
    other_down = lax.ppermute(down_own, "y", pairs)
    up, down = along_z(mine, 1), along_z(mine, -1)
    split = micro * tok
    far = (along_z(down[:split], -1), along_z(up[split:], 1))

    place = jnp.full((1,), my_z, jnp.int32)
    pick, scale, back, w_high, w_low = route(place, mine, up, far[0], down, plane * count)
    rows = select(pick, mine, up, far[0], down, plane)
    rows = select(pick, mine, up, far[1], down, plane, scale, rows)
    rows, other_gate, other_down = lax.optimization_barrier((rows, other_gate, other_down))
    other_gate = jnp.concatenate(other_gate, axis=1)
    rows = in_plane(rows)

    expert_out = forward(rows, weights)
    back_out = in_plane(expert_out.reshape(plane, count, width)).reshape(plane * count, width)
    row_input = backward(rows, weights)
    back_out, row_input = lax.optimization_barrier((back_out, row_input))
    back_grad = in_plane(row_input.reshape(plane, count, width)).reshape(plane * count, width)
    resident_gate = jnp.where(flag == 1, other_gate, gate_up)
    resident_down = jnp.where(flag == 1, other_down, down_t)

    results = []
    for factors, moved in (((w_high, w_low), back_out), ((back,), back_grad)):
        own, *others = combine(factors, moved)
        came = [along_z(others[s - 1], -s) for s in (2, 1, 3)]
        for part in came:
            own = own + part.astype(F32)
        results.append(own.astype(BF).reshape(micro, tok, width))
    return (results[0], results[1], resident_gate, resident_down)


def solution(mesh):
    devices = mesh.devices.reshape(4, 4, 4, 4, 2)
    fine = Mesh(devices, ("dp", "y", "x", "z", "c"))
    tokens = P(None, ("dp",) + EXPERT, None)
    placed = (
        tokens,
        tokens,
        tokens,
        tokens,
        P(),
        P(EXPERT, "dp", None, None),
        P(EXPERT, "dp", None),
    )
    return jax.shard_map(
        local,
        mesh=fine,
        in_specs=placed,
        out_specs=(tokens, tokens, P(EXPERT, "dp", None, None), P(EXPERT, "dp", None)),
        check_vma=False,
    )
```

```python
import functools

import jax
import jax.numpy as jnp
from jax import lax
from jax.experimental import pallas as pl
from jax.experimental.pallas import tpu as pltpu
from jax.sharding import Mesh, PartitionSpec as P

EXPERT = ("y", "x", "z", "c")
PLANE = ("y", "x", "c")
BF = jnp.bfloat16
F32 = jnp.float32
STEP = 512
MORE = 128
ROWS = 256
GRANT = 60 << 20
LAST = (((1,), (1,)), ((), ()))


def along_z(value, shift):
    count = lax.axis_size("z")
    return lax.ppermute(value, "z", [(i, (i + shift) % count) for i in range(count)])


def cost(flops, size):
    return pl.CostEstimate(flops=flops, bytes_accessed=size, transcendentals=0)


def route_body(place_ref, f0, f1, f2, f3, pick_ref, scale_ref, back_ref, high_ref, low_ref):
    n, slots = back_ref.shape
    facts = jnp.concatenate([f[...] for f in (f0, f1, f2, f3)], axis=0).astype(F32)
    ids = facts[:, 0:8].astype(jnp.int32)
    prob = facts[:, 8:16] + facts[:, 16:24] + facts[:, 24:32]
    place = jnp.where(((ids >> 1) & 3) == place_ref[0], ((ids >> 3) << 1) + (ids & 1), -1)
    col = lax.broadcasted_iota(jnp.int32, (n, slots), 1)
    row = lax.broadcasted_iota(jnp.int32, (n, slots), 0)
    dest = col >> 4
    hit = jnp.zeros((n, slots), jnp.bool_)
    weight = jnp.zeros((n, slots), F32)
    for k in range(8):
        same = place[:, k : k + 1] == dest
        hit = hit | same
        weight = jnp.where(same, prob[:, k : k + 1], weight)
    r2 = lax.broadcasted_iota(jnp.int32, (n, n), 0)
    c2 = lax.broadcasted_iota(jnp.int32, (n, n), 1)
    below = ((c2 < r2) & ((c2 >> 4) == (r2 >> 4))).astype(F32).astype(BF)
    earlier = jnp.dot(below, hit.astype(F32).astype(BF), preferred_element_type=F32)
    block = ((row >> 5) == ((col >> 1) & 3)) & (((row >> 4) & 1) == ((col >> 3) & 1))
    pick = hit & block & (earlier == (col & 1).astype(F32))
    pick_f = pick.astype(F32)
    scaled = jnp.where(pick, weight, 0.0)
    back_ref[...] = pick_f.astype(BF)
    high = scaled.astype(BF)
    high_ref[...] = high
    low_ref[...] = (scaled - high.astype(F32)).astype(BF)
    pick_ref[...] = jnp.transpose(pick_f).astype(BF)
    scale_ref[...] = jnp.sum(jnp.transpose(scaled), axis=1, keepdims=True)


def route(place, mine, up, far, down, slots):
    tokens = mine.shape[0]
    n = tokens * 4
    last = mine.shape[1] // MORE - 1
    facts = pl.BlockSpec((tokens, MORE), lambda i: (0, last))

    def whole(a, b):
        return pl.BlockSpec((a, b), lambda i: (0, 0))

    return pl.pallas_call(
        route_body,
        grid=(1,),
        in_specs=[pl.BlockSpec(memory_space=pltpu.SMEM)] + [facts] * 4,
        out_specs=[whole(slots, n), whole(slots, 1)] + [whole(n, slots)] * 3,
        out_shape=[jax.ShapeDtypeStruct((slots, n), BF), jax.ShapeDtypeStruct((slots, 1), F32)]
        + [jax.ShapeDtypeStruct((n, slots), BF)] * 3,
        compiler_params=pltpu.CompilerParams(vmem_limit_bytes=16 << 20),
        cost_estimate=cost(1 << 26, 1 << 20),
    )(place, mine, up, far, down)


def select_tokens_body(pick_ref, a0, a1, a2, a3, rows_ref):
    tokens = jnp.concatenate([a[...] for a in (a0, a1, a2, a3)], axis=0)
    rows = jnp.dot(pick_ref[...], tokens, preferred_element_type=F32)
    rows_ref[...] = rows.astype(BF).reshape(rows_ref.shape)


def select_grads_body(pick_ref, scale_ref, a0, a1, a2, a3, _, rows_ref):
    tokens = jnp.concatenate([a[...] for a in (a0, a1, a2, a3)], axis=0)
    rows = jnp.dot(pick_ref[...], tokens, preferred_element_type=F32)
    rows_ref[...] = (rows * scale_ref[...]).astype(BF).reshape(rows_ref.shape)


def select(pick, column, width, plane, scale=None, rows=None):
    slots, n = pick.shape
    part = n // 4
    which = 0 if rows is None else 1
    step = 2 * STEP
    whole = pl.BlockSpec((slots, n), lambda j: (0, 0))
    specs = [pl.BlockSpec((part, step), lambda j: (0, j))] * 4
    if which:
        specs = [whole, pl.BlockSpec((slots, 1), lambda j: (0, 0)), *specs, pl.BlockSpec(memory_space=pl.ANY)]
        operands = (pick, scale, *column, rows)
    else:
        specs = [whole, *specs]
        operands = (pick, *column)
    return pl.pallas_call(
        select_grads_body if which else select_tokens_body,
        grid=(width // step,),
        in_specs=specs,
        out_specs=pl.BlockSpec((plane, None, slots // plane, step), lambda j: (0, which, 0, j)),
        out_shape=jax.ShapeDtypeStruct((plane, 2, slots // plane, width), BF),
        input_output_aliases={len(operands) - 1: 0} if which else {},
        compiler_params=pltpu.CompilerParams(vmem_limit_bytes=GRANT),
        cost_estimate=cost(1 << 29, 3 << 20),
    )(*operands)


def forward_body(rows_hbm, weights_hbm, out_hbm, x_ref, w_ref, out_ref, came, went):
    plane, _, count, width = rows_hbm.shape
    hid = w_ref.shape[2] // 3
    steps = width // STEP

    def taken(k):
        columns = pl.ds(k * STEP, STEP)
        return (
            pltpu.make_async_copy(rows_hbm.at[:, 0, :, columns], x_ref.at[k], came.at[2 * k]),
            pltpu.make_async_copy(weights_hbm.at[columns], w_ref.at[k], came.at[2 * k + 1]),
        )

    def given(k):
        return pltpu.make_async_copy(out_ref.at[k], out_hbm.at[:, pl.ds(k * STEP, STEP)], went.at[k])

    for k in range(steps):
        for copy in taken(k):
            copy.start()
    projected = None
    for k in range(steps):
        for copy in taken(k):
            copy.wait()
        x = x_ref[k].reshape(plane * count, STEP)
        term = jnp.dot(x, w_ref[k, :, : 2 * hid], preferred_element_type=F32)
        projected = term if projected is None else projected + term
    gate_part = projected[:, :hid]
    hidden = (gate_part * jax.nn.sigmoid(gate_part) * projected[:, hid:]).astype(BF)
    for k in range(steps):
        out = lax.dot_general(hidden, w_ref[k, :, 2 * hid :], LAST, preferred_element_type=F32)
        out_ref[k] = out.astype(BF)
        given(k).start()
    for k in range(steps):
        given(k).wait()


def forward(rows, weights):
    plane, _, count, width = rows.shape
    total, steps = plane * count, width // STEP
    anywhere = pl.BlockSpec(memory_space=pl.ANY)
    return pl.pallas_call(
        forward_body,
        in_specs=[anywhere, anywhere],
        out_specs=anywhere,
        out_shape=jax.ShapeDtypeStruct((total, width), BF),
        scratch_shapes=[
            pltpu.VMEM((steps, plane, count, STEP), BF),
            pltpu.VMEM((steps, STEP, weights.shape[1]), BF),
            pltpu.VMEM((steps, total, STEP), BF),
            pltpu.SemaphoreType.DMA((2 * steps,)),
            pltpu.SemaphoreType.DMA((steps,)),
        ],
        compiler_params=pltpu.CompilerParams(vmem_limit_bytes=GRANT),
        cost_estimate=cost(5 << 29, 10 << 20),
    )(rows, weights)


def backward_body(x_ref, g_ref, w_ref, out_ref):
    hid = w_ref.shape[1] // 3
    x = x_ref[...].reshape(out_ref.shape)
    g = g_ref[...].reshape(out_ref.shape)
    projected = jnp.dot(x, w_ref[:, : 2 * hid], preferred_element_type=F32)
    d_hidden = jnp.dot(g, w_ref[:, 2 * hid :], preferred_element_type=F32)
    gate_part = projected[:, :hid]
    sig = jax.nn.sigmoid(gate_part)
    d_gate = d_hidden * projected[:, hid:] * sig * (1.0 + gate_part * (1.0 - sig))
    d_upper = d_hidden * gate_part * sig
    d_joined = jnp.concatenate([d_gate.astype(BF), d_upper.astype(BF)], axis=1)
    for j in range(0, out_ref.shape[1], STEP):
        out = lax.dot_general(d_joined, w_ref[j : j + STEP, : 2 * hid], LAST, preferred_element_type=F32)
        out_ref[:, j : j + STEP] = out.astype(BF)


def backward(rows, weights):
    plane, _, count, width = rows.shape
    total = plane * count

    def taken(which):
        return pl.BlockSpec((ROWS // count, None, count, width), lambda i: (i, which, 0, 0))

    return pl.pallas_call(
        backward_body,
        grid=(total // ROWS,),
        in_specs=[
            taken(0),
            taken(1),
            pl.BlockSpec(weights.shape, lambda i: (0, 0), pipeline_mode=pl.Buffered(1)),
        ],
        out_specs=pl.BlockSpec((ROWS, width), lambda i: (i, 0)),
        out_shape=jax.ShapeDtypeStruct((total, width), BF),
        compiler_params=pltpu.CompilerParams(vmem_limit_bytes=GRANT),
        cost_estimate=cost(7 << 29, 10 << 20),
    )(rows, rows, weights)


def combine_body(count, *refs):
    factors, rows, own_ref = refs[:count], refs[count][...], refs[count + 1]
    total = jnp.dot(factors[0][...], rows, preferred_element_type=F32)
    for f in factors[1:]:
        total = total + jnp.dot(f[...], rows, preferred_element_type=F32)
    m = own_ref.shape[0]
    own_ref[...] = total[:m]
    for s, ref in enumerate(refs[count + 2 :], 1):
        ref[...] = total[s * m : (s + 1) * m].astype(BF)


def combine(factors, rows):
    n, slots = factors[0].shape
    width = rows.shape[1]
    part = pl.BlockSpec((n // 4, STEP), lambda j: (0, j))
    return pl.pallas_call(
        functools.partial(combine_body, len(factors)),
        grid=(width // STEP,),
        in_specs=[pl.BlockSpec((n, slots), lambda j: (0, 0))] * len(factors)
        + [pl.BlockSpec((slots, STEP), lambda j: (0, j))],
        out_specs=[part] * 4,
        out_shape=[jax.ShapeDtypeStruct((n // 4, width), F32)]
        + [jax.ShapeDtypeStruct((n // 4, width), BF)] * 3,
        compiler_params=pltpu.CompilerParams(vmem_limit_bytes=16 << 20),
        cost_estimate=cost(1 << 28, 3 << 20),
    )(*factors, rows)


def in_plane(rows):
    return lax.all_to_all(rows, PLANE, 0, 0, tiled=True)


def local(hidden_in, cotangent, expert_ids, route_prob, swap_flags, gate_up, down_t):
    micro, tok, width = hidden_in.shape
    top = expert_ids.shape[2]
    hid = down_t.shape[2]
    nz = lax.axis_size("z")
    ny = lax.axis_size("y")
    plane = ny * lax.axis_size("x") * 2
    count = micro * nz * 2
    my_z = lax.axis_index("z")
    half = ny * lax.axis_size("x") * nz
    my_index = lax.axis_index(EXPERT)

    weights = jnp.concatenate([gate_up.reshape(-1, 2 * hid), down_t.reshape(-1, hid)], axis=1)
    weights = lax.all_gather(weights, "dp", axis=0, tiled=True)

    flag = jnp.sum(jnp.where(jnp.arange(half, dtype=jnp.int32) == my_index % half, swap_flags, 0))
    pairs = [(i, i ^ (ny // 2)) for i in range(ny)]

    high = lax.reduce_precision(route_prob, 8, 7)
    middle = lax.reduce_precision(route_prob - high, 8, 7)
    low = route_prob - high - middle
    facts = jnp.concatenate([expert_ids.astype(F32), high, middle, low], axis=2).astype(BF)
    facts = jnp.pad(facts.reshape(micro * tok, 4 * top), ((0, 0), (0, MORE - 4 * top)))
    mine = jnp.concatenate([hidden_in.reshape(micro * tok, width), facts], axis=1)
    mine_g = cotangent.reshape(micro * tok, width)
    gate_own, down_own, mine = lax.optimization_barrier((gate_up, down_t, mine))
    other_gate = [lax.ppermute(part, "y", pairs) for part in jnp.split(gate_own, 2, axis=1)]
    other_down = lax.ppermute(down_own, "y", pairs)
    down, up = along_z(mine, -1), along_z(mine, 1)
    up_g, down_g = along_z(mine_g, 1), along_z(mine_g, -1)
    far, far_g = along_z(down, -1), along_z(up_g, 1)

    place = jnp.full((1,), my_z, jnp.int32)
    pick, scale, back, w_high, w_low = route(place, mine, up, far, down, plane * count)
    rows = select(pick, (mine, up, far, down), width, plane)
    rows = select(pick, (mine_g, up_g, far_g, down_g), width, plane, scale, rows)
    rows, other_gate, other_down = lax.optimization_barrier((rows, other_gate, other_down))
    other_gate = jnp.concatenate(other_gate, axis=1)
    rows = in_plane(rows)

    expert_out = forward(rows, weights)
    back_out = in_plane(expert_out.reshape(plane, count, width)).reshape(plane * count, width)
    row_input = backward(rows, weights)
    back_out, row_input = lax.optimization_barrier((back_out, row_input))
    back_grad = in_plane(row_input.reshape(plane, count, width)).reshape(plane * count, width)
    resident_gate = jnp.where(flag == 1, other_gate, gate_up)
    resident_down = jnp.where(flag == 1, other_down, down_t)

    results = []
    for factors, moved in (((w_high, w_low), back_out), ((back,), back_grad)):
        own, *others = combine(factors, moved)
        came = [along_z(others[s - 1], -s) for s in (2, 1, 3)]
        for part in came:
            own = own + part.astype(F32)
        results.append(own.astype(BF).reshape(micro, tok, width))
    return (results[0], results[1], resident_gate, resident_down)


def solution(mesh):
    devices = mesh.devices.reshape(4, 4, 4, 4, 2)
    fine = Mesh(devices, ("dp", "y", "x", "z", "c"))
    tokens = P(None, ("dp",) + EXPERT, None)
    placed = (
        tokens,
        tokens,
        tokens,
        tokens,
        P(),
        P(EXPERT, "dp", None, None),
        P(EXPERT, "dp", None),
    )
    return jax.shard_map(
        local,
        mesh=fine,
        in_specs=placed,
        out_specs=(tokens, tokens, P(EXPERT, "dp", None, None), P(EXPERT, "dp", None)),
        check_vma=False,
    )
```
